32 devices in a mesh: section: 2 (over core), dp: 4 (over y, x), expert: 4 (over z).
Axes of the slice: x: 2, y: 2, z: 4, core: 2. Of those that a mesh axis runs over, the one named last changes fastest.
Arguments:
- tokens: bfloat16 [2, 64, 2048], P('section', 'expert'), may hold values from -6 to 6
- out_grad: bfloat16 [2, 64, 2048], P('section', 'expert'), may hold values from -6 to 6
- expert_ids: int32 [2, 64, 8], P('section', 'expert'), may hold values from 0 to 63, all different within a row; in each aligned block of 16 rows (0 to 15, 16 to 31, ..., all dimensions but the last counted through in order) at most 3 rows name the same one
- gates: bfloat16 [2, 64, 8], P('section', 'expert'), may hold values from 0.049804688 to 0.59765625
- w_gate: bfloat16 [2, 64, 2048, 1024], P('section', 'expert', None, 'dp'), may hold values from -0.125 to 0.125
- w_up: bfloat16 [2, 64, 2048, 1024], P('section', 'expert', None, 'dp'), may hold values from -0.125 to 0.125
- w_down: bfloat16 [2, 64, 1024, 2048], P('section', 'expert', 'dp'), may hold values from -0.1875 to 0.1875
Outputs:
- prev_grad: bfloat16 [2, 64, 2048], P('section', 'expert', 'dp')
- gate_grad: float32 [2, 64, 8], P('section', 'expert', 'dp')
- grad_w_gate: bfloat16 [2, 64, 2048, 1024], P('section', 'expert', None, 'dp')
- grad_w_up: bfloat16 [2, 64, 2048, 1024], P('section', 'expert', None, 'dp')
- grad_w_down: bfloat16 [2, 64, 1024, 2048], P('section', 'expert', 'dp')
The draws below stay inside these ranges and needn't reach their ends.
Inputs may be any that keep to these rules, and one draw needn't show every extreme that they name: `expert_ids`: each token names 8 different experts; within one section, the 16 tokens of one index of expert name any one expert at most 3 times.
All inputs are finite; a program needn't handle non-finite values.
Results may differ from the reference program's by a relative error of at most 0.0057.
Values may be sent and summed in bfloat16 or wider, within the bound.
A program may use at most 192 MiB of HBM per device.

```python
import math
import jax
import jax.numpy as jnp
import numpy as np
from jax import lax

D = 2048
FF = 1024
TOP = 8
EXPERTS = 64
TOK_DEV = 16
CAP = 3
TOKENS = 64
SECTIONS = 2
N_SECTION = 2
N_EXPERT = 4


def levels(rng, extent, cuts, smallest, top_value):
    def one(position, blocks):
        steps = jax.random.uniform(jax.random.fold_in(jax.random.fold_in(rng, 6), position), (blocks,), jnp.float32, smallest / len(cuts), top_value / len(cuts))
        return jnp.repeat(jnp.exp(steps), extent[position] // blocks).reshape((-1,) + (1,) * (len(extent) - position - 1))

    factor_of = one(*cuts[0])
    for cut in cuts[1:]:
        factor_of = factor_of * one(*cut)
    return factor_of


def shared_out(key, own, number, rows, amount, top, limit, skew):
    sequence = jax.random.permutation(key, amount)
    heavy_load, ordinary = portions_of(amount, rows * top, limit, skew, True), portions_of(amount, rows * top, limit, skew, False)
    places = jnp.arange(amount)

    def named(sizes, rotation):
        used = int((sizes > 0).sum())
        fixed = max(1, used // 4)
        shifted = fixed + (places - fixed + rotation * (used - fixed)) % max(1, amount - fixed)
        return jnp.zeros((amount,), jnp.int32).at[sequence[jnp.where(places < fixed, places, shifted)]].set(jnp.asarray(sizes, jnp.int32))

    sizes = jnp.where(number % 4 == 0, named(heavy_load, number // 4), named(ordinary, number - number // 4 - 1))
    mixed = jax.random.permutation(jax.random.fold_in(own, 3), amount)
    giver, sink = mixed[0:amount // 2 * 2:2], mixed[1:amount // 2 * 2:2]
    margin = jnp.minimum(sizes[giver] - 1, limit - sizes[sink]) // 2
    margin = jnp.where((giver == sequence[0]) | (sink == sequence[0]) | (sizes[sink] == 0), 0, jnp.maximum(margin, 0))
    shifted = jax.random.randint(jax.random.fold_in(own, 4), (amount // 2,), 0, 1 << 20) % (margin + 1)
    sizes = sizes.at[giver].add(-shifted).at[sink].add(shifted)
    labels = jnp.searchsorted(jnp.cumsum(sizes), jnp.arange(rows * top), side="right").astype(jnp.int32)
    listing = labels.reshape(top, rows).T
    listing = listing[jax.random.permutation(jax.random.fold_in(own, 1), rows)]
    rotation = jax.random.randint(jax.random.fold_in(own, 2), (rows, 1), 0, top)
    return jnp.take_along_axis(listing, (jnp.arange(top)[None, :] + rotation) % top, axis=1)


def portions_of(count, total, reach, slope, full):
    weights = [(1 << 20) // math.isqrt(standing ** slope) + 1 for standing in range(1, count + 1)]
    largest = reach if full else min(reach, max(-(-total // count), total * weights[0] // sum(weights)))
    least = 1 if total - largest >= count - 1 else 0
    holding, rest = [largest] + [least] * (count - 1), total - largest - least * (count - 1)
    while rest > 0:
        candidates = [i for i in range(1, count) if holding[i] < largest] or [i for i in range(1, count) if holding[i] < reach]
        mass, left = sum([weights[i] for i in candidates]), rest
        for i in candidates:
            more = min(reach - holding[i], max(1, left * weights[i] // mass), rest)
            holding[i] = holding[i] + more
            rest = rest - more
    return np.array(holding)


def gaussian(key, extent, scale, bound, cuts=(), kind=jnp.bfloat16):
    entries = jax.random.normal(key, extent, jnp.float32) * scale
    if len(cuts) > 0:
        entries = levels(key, extent, cuts, -0.22, 0.18) * entries
    return jnp.clip(entries, min=-bound, max=bound).astype(kind)


def setup_inputs(seed: int = 0) -> dict:
    keys = jax.random.split(jax.random.key(seed), 8)
    tokens = gaussian(keys[0], (SECTIONS, TOKENS, D), 1.0, 6.0, ((0, 2), (1, 4)))
    out_grad = gaussian(keys[1], (SECTIONS, TOKENS, D), 1.0, 6.0, ((0, 2), (1, 4)))
    expert_ids_keys = jax.random.split(jax.random.fold_in(keys[2], 1), SECTIONS * TOKENS // TOK_DEV)
    expert_ids_turns = jax.random.permutation(jax.random.fold_in(keys[2], 3), SECTIONS * TOKENS // TOK_DEV)
    expert_ids = jax.vmap(lambda own, number: shared_out(jax.random.fold_in(keys[2], 2), own, number, TOK_DEV, EXPERTS, TOP, CAP, 2))(expert_ids_keys, expert_ids_turns).reshape((SECTIONS, TOKENS, TOP))
    gates = jnp.clip(0.049804688 + 0.54785156 * jax.random.uniform(keys[3], (SECTIONS, TOKENS, TOP), jnp.float32) ** levels(keys[3], (SECTIONS, TOKENS, TOP), ((0, 2), (1, 4)), -0.2, 0.2), 0.049804688, 0.59765625).astype(jnp.bfloat16)
    w_gate = gaussian(keys[4], (SECTIONS, EXPERTS, D, FF), D ** -0.5, 0.125, ((0, 2), (1, 4), (3, 4)))
    w_up = gaussian(keys[5], (SECTIONS, EXPERTS, D, FF), D ** -0.5, 0.125, ((0, 2), (1, 4), (3, 4)))
    w_down = gaussian(keys[6], (SECTIONS, EXPERTS, FF, D), FF ** -0.5, 0.1875, ((0, 2), (1, 4), (2, 4)))
    return dict(tokens=tokens, out_grad=out_grad, expert_ids=expert_ids, gates=gates, w_gate=w_gate, w_up=w_up, w_down=w_down)


def expert_backward(xs, dys, gs, wg, wu, wd):
    a = jnp.dot(xs, wg, preferred_element_type=jnp.float32)
    b = jnp.dot(xs, wu, preferred_element_type=jnp.float32)
    sig = jax.nn.sigmoid(a)
    silu = a * sig
    hid = silu * b
    dz = jnp.dot(dys, wd.T, preferred_element_type=jnp.float32)
    gate_f = gs.astype(jnp.float32)[:, None]
    dgate = jnp.sum(hid * dz, axis=1)
    dh = gate_f * dz
    db = (dh * silu).astype(jnp.bfloat16)
    da = (dh * b * sig * (1.0 + a * (1.0 - sig))).astype(jnp.bfloat16)
    hid_b = hid.astype(jnp.bfloat16)
    dout = (gate_f * dys.astype(jnp.float32)).astype(jnp.bfloat16)
    dwg = jnp.dot(xs.T, da, preferred_element_type=jnp.float32)
    dwu = jnp.dot(xs.T, db, preferred_element_type=jnp.float32)
    dwd = jnp.dot(hid_b.T, dout, preferred_element_type=jnp.float32)
    dxp = jnp.dot(da, wg.T, preferred_element_type=jnp.float32) + jnp.dot(db, wu.T, preferred_element_type=jnp.float32)
    return dxp, dgate, dwg, dwu, dwd


def slot_table(ids):
    flat = ids.reshape(N_EXPERT, TOK_DEV * TOP)
    onehot = (flat[:, :, None] == jnp.arange(EXPERTS, dtype=jnp.int32)[None, None, :]).astype(jnp.int32)
    rank = jnp.sum((jnp.cumsum(onehot, axis=1) - onehot) * onehot, axis=2).astype(jnp.int32)
    source = jnp.arange(N_EXPERT, dtype=jnp.int32)[:, None]
    column = source * CAP + rank
    pairs = jnp.arange(TOKENS * TOP, dtype=jnp.int32).reshape(N_EXPERT, TOK_DEV * TOP)
    table = jnp.full((EXPERTS, N_EXPERT * CAP), -1, jnp.int32)
    return table.at[flat, column].set(pairs)


def reference(tokens, out_grad, expert_ids, gates, w_gate, w_up, w_down):
    grads_x = []
    grads_g = []
    grads_wg = []
    grads_wu = []
    grads_wd = []
    for section_idx in range(N_SECTION):
        x_section = tokens[section_idx]
        dy_section = out_grad[section_idx]
        gate_flat = gates[section_idx].reshape(-1)
        table = slot_table(expert_ids[section_idx])

        def per_expert(operands):
            rows, wg, wu, wd = operands
            valid = rows >= 0
            pair = jnp.maximum(rows, 0).astype(jnp.int32)
            tok = (pair // TOP).astype(jnp.int32)
            xs = jnp.where(valid[:, None], x_section[tok], jnp.zeros((), jnp.bfloat16))
            dys = jnp.where(valid[:, None], dy_section[tok], jnp.zeros((), jnp.bfloat16))
            gs = jnp.where(valid, gate_flat[pair], jnp.zeros((), jnp.bfloat16))
            return expert_backward(xs, dys, gs, wg, wu, wd)

        dxp, dgp, dwg, dwu, dwd = lax.map(per_expert, (table, w_gate[section_idx], w_up[section_idx], w_down[section_idx]))
        rows_all = table.reshape(-1)
        valid_all = rows_all >= 0
        pair_all = jnp.maximum(rows_all, 0).astype(jnp.int32)
        tok_all = (pair_all // TOP).astype(jnp.int32)
        dx_terms = jnp.where(valid_all[:, None], dxp.reshape(-1, D), jnp.zeros((), jnp.float32))
        dx_section = jnp.zeros((TOKENS, D), jnp.float32).at[tok_all].add(dx_terms)
        dg_terms = jnp.where(valid_all, dgp.reshape(-1), jnp.zeros((), jnp.float32))
        dg_section = jnp.zeros((TOKENS * TOP,), jnp.float32).at[pair_all].add(dg_terms)
        grads_x.append(dx_section)
        grads_g.append(dg_section.reshape(TOKENS, TOP))
        grads_wg.append(dwg.astype(jnp.bfloat16))
        grads_wu.append(dwu.astype(jnp.bfloat16))
        grads_wd.append(dwd.astype(jnp.bfloat16))
    stacked = jnp.stack(grads_x)
    prev_grad = jnp.roll(stacked, -1, axis=0).astype(jnp.bfloat16)
    return (prev_grad, jnp.stack(grads_g), jnp.stack(grads_wg), jnp.stack(grads_wu), jnp.stack(grads_wd))
```

```python
import functools

import jax
import jax.numpy as jnp
from jax import lax
from jax.experimental import pallas as pl
from jax.experimental.pallas import tpu as pltpu
from jax.sharding import PartitionSpec as P

BF = jnp.bfloat16
F32 = jnp.float32
MESH = pl.DeviceIdType.MESH
VMEM = pl.BlockSpec(memory_space=pltpu.VMEM)
LIMIT = 60 * 1024 * 1024


def each(start, stop, body):
    if stop - start <= 8:
        for i in range(start, stop):
            body(i)
    else:
        lax.fori_loop(start, stop, lambda i, c: (body(i), c)[1], 0)


def signal(barrier, where):
    pl.semaphore_signal(barrier, inc=1, device_id=where, device_id_type=MESH)


def push(src, dst, send, recv, where):
    return pltpu.make_async_remote_copy(
        src_ref=src, dst_ref=dst, send_sem=send, recv_sem=recv, device_id=where, device_id_type=MESH
    )


def gather_kernel(n, ndp, x_ref, dy_ref, ids_ref, gates_ref, xy_ref, g_ref, s1, r1, sg, rg, s2, r2):
    me = lax.axis_index("expert")
    d = lax.axis_index("dp")
    rows, width = x_ref.shape
    top = ids_ref.shape[1]
    lanes = g_ref.shape[2]
    part = width // ndp
    barrier = pltpu.get_barrier_semaphore()
    each(1, n, lambda o: signal(barrier, {"expert": lax.rem(me + o, n)}))
    each(1, ndp, lambda o: signal(barrier, {"dp": lax.rem(d + o, ndp)}))

    mine = pl.ds(pl.multiple_of(me * rows, rows), rows)
    xy_ref[0, mine, :] = x_ref[...]
    xy_ref[1, mine, :] = dy_ref[...]
    lane = lax.broadcasted_iota(jnp.int32, (rows, lanes), 1)
    ids = ids_ref[...]
    gates = gates_ref[...].astype(F32)
    g = jnp.zeros((rows, lanes), F32)
    for k in range(top):
        g = g + jnp.where(lane == ids[:, k : k + 1], gates[:, k : k + 1], 0.0)
    g_ref[me] = g
    pl.semaphore_wait(barrier, n - 1 + ndp - 1)

    cols = pl.ds(pl.multiple_of(d * part, 128), part)

    def block(e):
        return xy_ref.at[:, pl.ds(pl.multiple_of(e * rows, rows), rows), cols]

    def along(o):
        to = {"expert": lax.rem(me + o, n)}
        return push(block(me), block(me), s1.at[o], r1.at[o], to)

    def gate(o):
        to = {"expert": lax.rem(me + o, n)}
        return push(g_ref.at[me], g_ref.at[me], sg.at[o], rg.at[o], to)

    def spread(o, q):
        e = lax.rem(me - o + n, n)
        to = {"dp": lax.rem(d + q, ndp)}
        return push(block(e), block(e), s2.at[o, q], r2.at[o, q], to)

    each(1, n, lambda o: along(o).start())
    each(1, n, lambda o: gate(o).start())

    def pass_on(o):
        along(o).wait_recv()
        each(1, ndp, lambda q: spread(o, q).start())

    each(1, n, pass_on)

    def finish(o):
        along(o).wait_send()
        gate(o).wait()
        each(1, ndp, lambda q: spread(o, q).wait())

    each(1, n, finish)


def gather(x, dy, ids, gates, n, ndp, lanes):
    rows, width = x.shape
    dma = pltpu.SemaphoreType.DMA
    return pl.pallas_call(
        functools.partial(gather_kernel, n, ndp),
        out_shape=(
            jax.ShapeDtypeStruct((2, n * rows, width), BF),
            jax.ShapeDtypeStruct((n, rows, lanes), F32),
        ),
        in_specs=[VMEM] * 4,
        out_specs=(VMEM, VMEM),
        scratch_shapes=[dma((n,)), dma((n,)), dma((n,)), dma((n,)), dma((n, ndp)), dma((n, ndp))],
        compiler_params=pltpu.CompilerParams(
            collective_id=0, has_side_effects=True, vmem_limit_bytes=LIMIT
        ),
        name="gather_tokens",
    )(x, dy, ids, gates)


def nt(a, b):
    return lax.dot_general(a, b, (((1,), (1,)), ((), ())), preferred_element_type=F32)


def nn(a, b):
    return jnp.dot(a, b, preferred_element_type=F32)


def expert_kernel(
    base_ref, xy_ref, g_ref, wg_ref, wu_ref, wd_ref, dx_ref, dg_ref, ogate, oup, odown, xt, acc, dgs
):
    e = pl.program_id(0)
    last = pl.num_programs(0) - 1
    tok = xy_ref.shape[1]
    width = xy_ref.shape[2]
    chunk = 256

    @pl.when(e == 0)
    def _():
        def turn(i, c):
            at = pl.ds(pl.multiple_of(i * chunk, chunk), chunk)
            xt[at, :] = xy_ref[0, :, at].T
            return c

        lax.fori_loop(0, width // chunk, turn, 0)
        acc[...] = jnp.zeros_like(acc)
        dgs[...] = jnp.zeros_like(dgs)

    lane = lax.broadcasted_iota(jnp.int32, g_ref.shape, 1)
    here = lane == e + base_ref[0]
    g = jnp.sum(jnp.where(here, g_ref[...], 0.0), axis=1, keepdims=True)
    x = xy_ref[0]
    dy = xy_ref[1]
    a = nn(x, wg_ref[0])
    b = nn(x, wu_ref[0])
    dz = nt(dy, wd_ref[0])
    sig = jax.nn.sigmoid(a)
    silu = a * sig
    hid = silu * b
    dgs[...] += jnp.where(here, jnp.sum(hid * dz, axis=1, keepdims=True), 0.0)
    dh = g * dz
    db = (dh * silu).astype(BF)
    da = (dh * b * sig * (1.0 + a * (1.0 - sig))).astype(BF)
    hid_t = hid.astype(BF).T

    for i in range(width // chunk):
        at = slice(i * chunk, (i + 1) * chunk)
        acc[:, at] += nt(da, wg_ref[0, at, :]) + nt(db, wu_ref[0, at, :])
        xc = xt[at, :]
        ogate[0, at, :] = nn(xc, da).astype(BF)
        oup[0, at, :] = nn(xc, db).astype(BF)
        dout = (g * xy_ref[1, :, at].astype(F32)).astype(BF)
        odown[0, :, at] = nn(hid_t, dout).astype(BF)

    @pl.when(e == last)
    def _():
        dx_ref[...] = acc[...].astype(BF)
        dg_ref[...] = dgs[...]


def experts(base, xy, g, wg, wu, wd):
    count, width, hidden = wg.shape
    tok = xy.shape[1]
    lanes = g.shape[1]
    whole = lambda *shape: pl.BlockSpec(shape, lambda e, b: (0,) * len(shape))
    one = lambda *shape: pl.BlockSpec((1,) + shape, lambda e, b: (e, 0, 0))
    return pl.pallas_call(
        expert_kernel,
        grid_spec=pltpu.PrefetchScalarGridSpec(
            num_scalar_prefetch=1,
            grid=(count,),
            in_specs=[
                whole(2, tok, width),
                whole(tok, lanes),
                one(width, hidden),
                one(width, hidden),
                one(hidden, width),
            ],
            out_specs=[
                whole(tok, width),
                whole(tok, lanes),
                one(width, hidden),
                one(width, hidden),
                one(hidden, width),
            ],
            scratch_shapes=[
                pltpu.VMEM((width, tok), BF),
                pltpu.VMEM((tok, width), F32),
                pltpu.VMEM((tok, lanes), F32),
            ],
        ),
        out_shape=(
            jax.ShapeDtypeStruct((tok, width), BF),
            jax.ShapeDtypeStruct((tok, lanes), F32),
            jax.ShapeDtypeStruct(wg.shape, BF),
            jax.ShapeDtypeStruct(wu.shape, BF),
            jax.ShapeDtypeStruct(wd.shape, BF),
        ),
        compiler_params=pltpu.CompilerParams(vmem_limit_bytes=LIMIT),
        name="experts",
    )(base, xy, g, wg, wu, wd)


def reduce_kernel(
    n, ndp, dx_ref, dg_ref, ids_ref, out_ref, gg_ref,
    rb, gb, sb, hb, rb2, gb2, s1, r1, sg, rg, s2, r2, sh, rh
):
    me = lax.axis_index("expert")
    d = lax.axis_index("dp")
    sec = lax.axis_index("section")
    nsec = lax.axis_size("section")
    to_sec = lax.rem(sec + nsec - 1, nsec)
    rows, part = out_ref.shape
    lanes = dg_ref.shape[1]
    barrier = pltpu.get_barrier_semaphore()
    each(1, ndp, lambda o: signal(barrier, {"dp": lax.rem(d + o, ndp)}))
    each(1, n, lambda o: signal(barrier, {"expert": lax.rem(me + o, n)}))
    each(0, n, lambda o: signal(barrier, {"section": to_sec, "expert": lax.rem(me + o, n)}))
    pl.semaphore_wait(barrier, ndp - 1 + n - 1 + n)

    def cols(p):
        return pl.ds(pl.multiple_of(p * part, 128), part)

    def first(o):
        p = lax.rem(d + o, ndp)
        return push(dx_ref.at[:, cols(p)], rb.at[o], s1.at[o], r1.at[o], {"dp": p})

    def first_g(o):
        p = lax.rem(d + o, ndp)
        return push(dg_ref, gb.at[o], sg.at[o], rg.at[o], {"dp": p})

    each(1, ndp, lambda o: first(o).start())
    each(1, ndp, lambda o: first_g(o).start())

    def wait_first(o):
        first_g(o).wait()
        first(o).wait()

    each(1, ndp, wait_first)

    def sums(e):
        at = pl.ds(pl.multiple_of(e * rows, rows), rows)
        t = dx_ref[at, cols(d)].astype(F32)
        u = dg_ref[at, :]
        for o in range(1, ndp):
            t = t + rb[o, at, :].astype(F32)
            u = u + gb[o, at, :]
        sb[e] = t
        hb[e] = u

    each(0, n, sums)

    def second(o):
        p = lax.rem(me + o, n)
        return push(sb.at[p], rb2.at[o], s2.at[o], r2.at[o], {"section": to_sec, "expert": p})

    def second_g(o):
        p = lax.rem(me + o, n)
        return push(hb.at[p], gb2.at[o], sh.at[o], rh.at[o], {"expert": p})

    each(0, n, lambda o: second(o).start())
    each(1, n, lambda o: second_g(o).start())
    each(1, n, lambda o: second_g(o).wait())
    each(0, n, lambda o: second(o).wait())
    out_ref[...] = jnp.sum(rb2[...], axis=0)

    if n <= 8:
        u = hb[me]
        for o in range(1, n):
            u = u + gb2[o]
    else:
        u = lax.fori_loop(1, n, lambda o, u: u + gb2[o], hb[me])
    ids = ids_ref[...]
    top = ids.shape[1]
    mine = gg_ref.shape[1]
    lane = lax.broadcasted_iota(jnp.int32, (rows, lanes), 1)
    spot = lax.broadcasted_iota(jnp.int32, (rows, mine), 1)
    res = jnp.zeros((rows, mine), F32)
    for k in range(top):
        v = jnp.sum(jnp.where(lane == ids[:, k : k + 1], u, 0.0), axis=1, keepdims=True)
        res = res + jnp.where(spot + d * mine == k, v, 0.0)
    gg_ref[...] = res


def reduce(dx, dg, ids, n, ndp):
    tok, width = dx.shape
    lanes = dg.shape[1]
    rows = tok // n
    part = width // ndp
    top = ids.shape[1]
    dma = pltpu.SemaphoreType.DMA
    return pl.pallas_call(
        functools.partial(reduce_kernel, n, ndp),
        out_shape=(
            jax.ShapeDtypeStruct((rows, part), F32),
            jax.ShapeDtypeStruct((rows, top // ndp), F32),
        ),
        in_specs=[VMEM] * 3,
        out_specs=(VMEM, VMEM),
        scratch_shapes=[
            pltpu.VMEM((ndp, tok, part), BF),
            pltpu.VMEM((ndp, tok, lanes), F32),
            pltpu.VMEM((n, rows, part), F32),
            pltpu.VMEM((n, rows, lanes), F32),
            pltpu.VMEM((n, rows, part), F32),
            pltpu.VMEM((n, rows, lanes), F32),
            dma((ndp,)), dma((ndp,)), dma((ndp,)), dma((ndp,)),
            dma((n,)), dma((n,)), dma((n,)), dma((n,)),
        ],
        compiler_params=pltpu.CompilerParams(
            collective_id=1, has_side_effects=True, vmem_limit_bytes=LIMIT
        ),
        name="reduce_dx",
    )(dx, dg, ids)


def local(tokens, out_grad, expert_ids, gates, w_gate, w_up, w_down):
    n = lax.axis_size("expert")
    ndp = lax.axis_size("dp")
    exp_loc = w_gate.shape[1]
    lanes = -(-exp_loc * n // 128) * 128
    xy, g = gather(tokens[0], out_grad[0], expert_ids[0], gates[0], n, ndp, lanes)
    base = (lax.axis_index("expert") * exp_loc).astype(jnp.int32).reshape(1)
    dx, dg, dwg, dwu, dwd = experts(
        base, xy, g.reshape(-1, lanes), w_gate[0], w_up[0], w_down[0]
    )
    prev, gg = reduce(dx, dg, expert_ids[0], n, ndp)
    return prev.astype(BF)[None], gg[None], dwg[None], dwu[None], dwd[None]


def solution(mesh):
    placed = (
        P("section", "expert", None),
        P("section", "expert", None),
        P("section", "expert", None),
        P("section", "expert", None),
        P("section", "expert", None, "dp"),
        P("section", "expert", None, "dp"),
        P("section", "expert", "dp", None),
    )
    return jax.shard_map(
        local,
        mesh=mesh,
        in_specs=placed,
        out_specs=(
            P("section", "expert", "dp"),
            P("section", "expert", "dp"),
            P("section", "expert", None, "dp"),
            P("section", "expert", None, "dp"),
            P("section", "expert", "dp", None),
        ),
        check_vma=False,
    )
```

```python
import functools

import jax
import jax.numpy as jnp
from jax import lax
from jax.experimental import pallas as pl
from jax.experimental.pallas import tpu as pltpu
from jax.sharding import PartitionSpec as P

BF = jnp.bfloat16
F32 = jnp.float32
MESH = pl.DeviceIdType.MESH
VMEM = pl.BlockSpec(memory_space=pltpu.VMEM)
LIMIT = 60 * 1024 * 1024


def each(start, stop, body):
    if stop - start <= 8:
        for i in range(start, stop):
            body(i)
    else:
        lax.fori_loop(start, stop, lambda i, c: (body(i), c)[1], 0)


def signal(barrier, where):
    pl.semaphore_signal(barrier, inc=1, device_id=where, device_id_type=MESH)


def push(src, dst, send, recv, where):
    return pltpu.make_async_remote_copy(
        src_ref=src, dst_ref=dst, send_sem=send, recv_sem=recv, device_id=where, device_id_type=MESH
    )


def columns_of(ref):
    v = ref[...].astype(F32)
    top = v.shape[0]
    one = lax.broadcasted_iota(jnp.int32, (top, top), 0)
    two = lax.broadcasted_iota(jnp.int32, (top, top), 1)
    eye = jnp.where(one == two, 1.0, 0.0)
    return lax.dot_general(
        v, eye, (((0,), (0,)), ((), ())), precision=lax.Precision.HIGHEST, preferred_element_type=F32
    )


def gather_kernel(n, ndp, x_ref, dy_ref, ids_ref, gates_ref, xy_ref, g_ref, s1, r1, sg, rg, s2, r2):
    me = lax.axis_index("expert")
    d = lax.axis_index("dp")
    rows, width = x_ref.shape
    top = ids_ref.shape[0]
    lanes = g_ref.shape[2]
    part = width // ndp
    barrier = pltpu.get_barrier_semaphore()
    each(1, n, lambda o: signal(barrier, {"expert": lax.rem(me + o, n)}))
    each(1, ndp, lambda o: signal(barrier, {"dp": lax.rem(d + o, ndp)}))

    mine = pl.ds(pl.multiple_of(me * rows, rows), rows)
    xy_ref[0, mine, :] = x_ref[...]
    xy_ref[1, mine, :] = dy_ref[...]
    lane = lax.broadcasted_iota(jnp.int32, (rows, lanes), 1).astype(F32)
    ids = columns_of(ids_ref)
    gates = columns_of(gates_ref)
    g = jnp.zeros((rows, lanes), F32)
    for k in range(top):
        g = g + jnp.where(lane == ids[:, k : k + 1], gates[:, k : k + 1], 0.0)
    g_ref[me] = g
    pl.semaphore_wait(barrier, n - 1 + ndp - 1)

    cols = pl.ds(pl.multiple_of(d * part, 128), part)

    def block(e):
        return xy_ref.at[:, pl.ds(pl.multiple_of(e * rows, rows), rows), cols]

    def along(o):
        to = {"expert": lax.rem(me + o, n)}
        return push(block(me), block(me), s1.at[o], r1.at[o], to)

    def gate(o):
        to = {"expert": lax.rem(me + o, n)}
        return push(g_ref.at[me], g_ref.at[me], sg.at[o], rg.at[o], to)

    def spread(o, q):
        e = lax.rem(me - o + n, n)
        to = {"dp": lax.rem(d + q, ndp)}
        return push(block(e), block(e), s2.at[o, q], r2.at[o, q], to)

    each(1, n, lambda o: along(o).start())
    each(1, n, lambda o: gate(o).start())

    def pass_on(o):
        along(o).wait_recv()
        each(1, ndp, lambda q: spread(o, q).start())

    each(1, n, pass_on)

    def finish(o):
        along(o).wait_send()
        gate(o).wait()
        each(1, ndp, lambda q: spread(o, q).wait())

    each(1, n, finish)


def gather(x, dy, ids, gates, n, ndp, lanes):
    rows, width = x.shape
    dma = pltpu.SemaphoreType.DMA
    return pl.pallas_call(
        functools.partial(gather_kernel, n, ndp),
        out_shape=(
            jax.ShapeDtypeStruct((2, n * rows, width), BF),
            jax.ShapeDtypeStruct((n, rows, lanes), F32),
        ),
        in_specs=[VMEM] * 4,
        out_specs=(VMEM, VMEM),
        scratch_shapes=[dma((n,)), dma((n,)), dma((n,)), dma((n,)), dma((n, ndp)), dma((n, ndp))],
        compiler_params=pltpu.CompilerParams(
            collective_id=0, has_side_effects=True, vmem_limit_bytes=LIMIT
        ),
        name="gather_tokens",
    )(x, dy, ids, gates)


def nt(a, b):
    return lax.dot_general(a, b, (((1,), (1,)), ((), ())), preferred_element_type=F32)


def nn(a, b):
    return jnp.dot(a, b, preferred_element_type=F32)


def expert_kernel(
    nin, nout, base_ref, xy_ref, g_ref, wg_ref, wu_ref, wd_ref, dx_ref, dg_ref, ogate, oup, odown,
    xt, acc, sda, sdb, sht, sg, bg, bu, bd, cg, cu, cd, sin, sout
):
    count, width, hidden = wg_ref.shape
    chunk = 256

    def load(e):
        slot = lax.rem(e, nin)
        pairs = ((wg_ref, bg), (wu_ref, bu), (wd_ref, bd))
        return [
            pltpu.make_async_copy(src.at[e], dst.at[slot], sin.at[i, slot])
            for i, (src, dst) in enumerate(pairs)
        ]

    def store(e):
        slot = lax.rem(e, nout)
        pairs = ((cg, ogate), (cu, oup), (cd, odown))
        return [
            pltpu.make_async_copy(src.at[slot], dst.at[e], sout.at[i, slot])
            for i, (src, dst) in enumerate(pairs)
        ]

    for e in range(nin):
        for c in load(e):
            c.start()

    def turn(i, c):
        at = pl.ds(pl.multiple_of(i * chunk, chunk), chunk)
        xt[at, :] = xy_ref[0, :, at].T
        return c

    lax.fori_loop(0, width // chunk, turn, 0)
    acc[...] = jnp.zeros_like(acc)
    dg_ref[...] = jnp.zeros_like(dg_ref)
    lane = lax.broadcasted_iota(jnp.int32, g_ref.shape, 1)

    def forward(e):
        for c in load(e):
            c.wait()
        k = lax.rem(e, nin)
        here = lane == e + base_ref[0]
        g = jnp.sum(jnp.where(here, g_ref[...], 0.0), axis=1, keepdims=True)
        a = nn(xy_ref[0], bg[k])
        b = nn(xy_ref[0], bu[k])
        dz = nt(xy_ref[1], bd[k])
        return here, g, a, b, dz

    def middle(here, g, a, b, dz):
        sig = jax.nn.sigmoid(a)
        silu = a * sig
        hid = silu * b
        dg_ref[...] += jnp.where(here, jnp.sum(hid * dz, axis=1, keepdims=True), 0.0)
        dh = g * dz
        sdb[...] = (dh * silu).astype(BF)
        sda[...] = (dh * b * sig * (1.0 + a * (1.0 - sig))).astype(BF)
        sht[...] = hid.astype(BF).T
        sg[...] = jnp.broadcast_to(g, sg.shape)

    def held():
        return sda[...], sdb[...], sht[...], sg[:, :1]

    def backward(e, da, db, hid_t, g):
        k = lax.rem(e, nin)
        o = lax.rem(e, nout)
        for i in range(width // chunk):
            at = slice(i * chunk, (i + 1) * chunk)
            xc = xt[at, :]
            acc[:, at] += nt(da, bg[k, at, :]) + nt(db, bu[k, at, :])
            cg[o, at, :] = nn(xc, da).astype(BF)
            cu[o, at, :] = nn(xc, db).astype(BF)
            dout = (g * xy_ref[1, :, at].astype(F32)).astype(BF)
            cd[o, :, at] = nn(hid_t, dout).astype(BF)

    def free(e):
        @pl.when(e >= nout)
        def _():
            for c in store(e - nout):
                c.wait()

    def expert(e, carry):
        free(e)
        old = held()
        new = forward(e + 1)
        backward(e, *old)
        middle(*new)
        for c in store(e):
            c.start()

        @pl.when(e + nin < count)
        def _():
            for c in load(e + nin):
                c.start()

        return carry

    middle(*forward(0))
    lax.fori_loop(0, count - 1, expert, 0)
    free(count - 1)
    backward(count - 1, *held())
    for c in store(count - 1):
        c.start()
    dx_ref[...] = acc[...].astype(BF)
    for e in range(count - nout, count):
        for c in store(e):
            c.wait()


def experts(base, xy, g, wg, wu, wd, nin=4, nout=3):
    count, width, hidden = wg.shape
    tok = xy.shape[1]
    lanes = g.shape[1]
    nin, nout = min(nin, count), min(nout, count)
    hbm = pl.BlockSpec(memory_space=pl.ANY)
    dma = pltpu.SemaphoreType.DMA
    return pl.pallas_call(
        functools.partial(expert_kernel, nin, nout),
        in_specs=[pl.BlockSpec(memory_space=pltpu.SMEM), VMEM, VMEM, hbm, hbm, hbm],
        out_specs=(VMEM, VMEM, hbm, hbm, hbm),
        scratch_shapes=[
            pltpu.VMEM((width, tok), BF),
            pltpu.VMEM((tok, width), F32),
            pltpu.VMEM((tok, hidden), BF),
            pltpu.VMEM((tok, hidden), BF),
            pltpu.VMEM((hidden, tok), BF),
            pltpu.VMEM((tok, 128), F32),
            pltpu.VMEM((nin, width, hidden), BF),
            pltpu.VMEM((nin, width, hidden), BF),
            pltpu.VMEM((nin, hidden, width), BF),
            pltpu.VMEM((nout, width, hidden), BF),
            pltpu.VMEM((nout, width, hidden), BF),
            pltpu.VMEM((nout, hidden, width), BF),
            dma((3, nin)),
            dma((3, nout)),
        ],
        out_shape=(
            jax.ShapeDtypeStruct((tok, width), BF),
            jax.ShapeDtypeStruct((tok, lanes), F32),
            jax.ShapeDtypeStruct(wg.shape, BF),
            jax.ShapeDtypeStruct(wu.shape, BF),
            jax.ShapeDtypeStruct(wd.shape, BF),
        ),
        compiler_params=pltpu.CompilerParams(vmem_limit_bytes=LIMIT),
        name="experts",
    )(base, xy, g, wg, wu, wd)


def reduce_kernel(
    n, ndp, dx_ref, dg_ref, ids_ref, out_ref, gg_ref,
    rb, gb, sb, hb, rb2, gb2, s1, r1, sg, rg, s2, r2, sh, rh
):
    me = lax.axis_index("expert")
    d = lax.axis_index("dp")
    sec = lax.axis_index("section")
    nsec = lax.axis_size("section")
    to_sec = lax.rem(sec + nsec - 1, nsec)
    rows, part = out_ref.shape
    lanes = dg_ref.shape[1]
    barrier = pltpu.get_barrier_semaphore()
    each(1, ndp, lambda o: signal(barrier, {"dp": lax.rem(d + o, ndp)}))
    each(1, n, lambda o: signal(barrier, {"expert": lax.rem(me + o, n)}))
    each(0, n, lambda o: signal(barrier, {"section": to_sec, "expert": lax.rem(me + o, n)}))
    pl.semaphore_wait(barrier, ndp - 1 + n - 1 + n)

    def cols(p):
        return pl.ds(pl.multiple_of(p * part, 128), part)

    def first(o):
        p = lax.rem(d + o, ndp)
        return push(dx_ref.at[:, cols(p)], rb.at[o], s1.at[o], r1.at[o], {"dp": p})

    def first_g(o):
        p = lax.rem(d + o, ndp)
        return push(dg_ref, gb.at[o], sg.at[o], rg.at[o], {"dp": p})

    each(1, ndp, lambda o: first(o).start())
    each(1, ndp, lambda o: first_g(o).start())

    def wait_first(o):
        first_g(o).wait()
        first(o).wait()

    each(1, ndp, wait_first)

    def sums(e):
        at = pl.ds(pl.multiple_of(e * rows, rows), rows)
        t = dx_ref[at, cols(d)].astype(F32)
        u = dg_ref[at, :]
        for o in range(1, ndp):
            t = t + rb[o, at, :].astype(F32)
            u = u + gb[o, at, :]
        sb[e] = t
        hb[e] = u

    each(0, n, sums)

    def second(o):
        p = lax.rem(me + o, n)
        return push(sb.at[p], rb2.at[o], s2.at[o], r2.at[o], {"section": to_sec, "expert": p})

    def second_g(o):
        p = lax.rem(me + o, n)
        return push(hb.at[p], gb2.at[o], sh.at[o], rh.at[o], {"expert": p})

    each(0, n, lambda o: second(o).start())
    each(1, n, lambda o: second_g(o).start())
    each(1, n, lambda o: second_g(o).wait())
    each(0, n, lambda o: second(o).wait())
    out_ref[...] = jnp.sum(rb2[...], axis=0)

    if n <= 8:
        u = hb[me]
        for o in range(1, n):
            u = u + gb2[o]
    else:
        u = lax.fori_loop(1, n, lambda o, u: u + gb2[o], hb[me])
    ids = columns_of(ids_ref)
    top = ids.shape[1]
    mine = gg_ref.shape[1]
    lane = lax.broadcasted_iota(jnp.int32, (rows, lanes), 1).astype(F32)
    spot = lax.broadcasted_iota(jnp.int32, (rows, mine), 1)
    res = jnp.zeros((rows, mine), F32)
    for k in range(top):
        v = jnp.sum(jnp.where(lane == ids[:, k : k + 1], u, 0.0), axis=1, keepdims=True)
        res = res + jnp.where(spot + d * mine == k, v, 0.0)
    gg_ref[...] = res


def reduce(dx, dg, ids, n, ndp):
    tok, width = dx.shape
    lanes = dg.shape[1]
    rows = tok // n
    part = width // ndp
    top = ids.shape[0]
    dma = pltpu.SemaphoreType.DMA
    return pl.pallas_call(
        functools.partial(reduce_kernel, n, ndp),
        out_shape=(
            jax.ShapeDtypeStruct((rows, part), F32),
            jax.ShapeDtypeStruct((rows, top // ndp), F32),
        ),
        in_specs=[VMEM] * 3,
        out_specs=(VMEM, VMEM),
        scratch_shapes=[
            pltpu.VMEM((ndp, tok, part), BF),
            pltpu.VMEM((ndp, tok, lanes), F32),
            pltpu.VMEM((n, rows, part), F32),
            pltpu.VMEM((n, rows, lanes), F32),
            pltpu.VMEM((n, rows, part), F32),
            pltpu.VMEM((n, rows, lanes), F32),
            dma((ndp,)), dma((ndp,)), dma((ndp,)), dma((ndp,)),
            dma((n,)), dma((n,)), dma((n,)), dma((n,)),
        ],
        compiler_params=pltpu.CompilerParams(
            collective_id=1, has_side_effects=True, vmem_limit_bytes=LIMIT
        ),
        name="reduce_dx",
    )(dx, dg, ids)


def local(tokens, out_grad, expert_ids, gates, w_gate, w_up, w_down):
    n = lax.axis_size("expert")
    ndp = lax.axis_size("dp")
    exp_loc = w_gate.shape[1]
    lanes = -(-exp_loc * n // 128) * 128
    xy, g = gather(tokens[0], out_grad[0], expert_ids[0].T, gates[0].T, n, ndp, lanes)
    base = (lax.axis_index("expert") * exp_loc).astype(jnp.int32).reshape(1)
    dx, dg, dwg, dwu, dwd = experts(
        base, xy, g.reshape(-1, lanes), w_gate[0], w_up[0], w_down[0]
    )
    prev, gg = reduce(dx, dg, expert_ids[0].T, n, ndp)
    return prev.astype(BF)[None], gg[None], dwg[None], dwu[None], dwd[None]


def solution(mesh):
    placed = (
        P("section", "expert", None),
        P("section", "expert", None),
        P("section", "expert", None),
        P("section", "expert", None),
        P("section", "expert", None, "dp"),
        P("section", "expert", None, "dp"),
        P("section", "expert", "dp", None),
    )
    return jax.shard_map(
        local,
        mesh=mesh,
        in_specs=placed,
        out_specs=(
            P("section", "expert", "dp"),
            P("section", "expert", "dp"),
            P("section", "expert", None, "dp"),
            P("section", "expert", None, "dp"),
            P("section", "expert", "dp", None),
        ),
        check_vma=False,
    )
```
